512 devices in a mesh: dom: 64 (over y, x, core), feat: 8 (over z).
Axes of the slice: x: 4, y: 8, z: 8, core: 2. Of those that a mesh axis runs over, the one named last changes fastest.
Arguments:
- features: bfloat16 [512, 196608], P('feat', 'dom'), may hold values from -16 to 16
- weights: bfloat16 [2, 512, 512], replicated, may hold values from -0.1875 to 0.1875
- tile_values: bfloat16 [4608, 128, 128], P('dom'), may hold values from 0 to 0.099609375
- tile_blocks: int32 [4608, 2], P('dom'), may hold values from 0 to 31
- tile_counts: int32 [64], P('dom'), may hold values from 36 to 72
- replica: int32 [64, 64, 16], P('dom'), may hold values from -1 to 3071, as said below
- cotangent: bfloat16 [512, 196608], P(None, ('dom', 'feat')), may hold values from -6 to 6
Outputs:
- output: bfloat16 [512, 196608], P(None, ('dom', 'feat'))
- feature_grad: bfloat16 [512, 196608], P('feat', 'dom')
- weight_grad: float32 [2, 512, 512], P(None, 'feat')
The draws below stay inside these ranges and needn't reach their ends.
Inputs may be any that keep to these rules, and one draw needn't show every extreme that they name: `tile_blocks`: column 0 names a tile's source block and column 1 its destination block. replica[q, p, k] is the master slot on partition q of the vertex in mirror slot q * 16 + k of partition p, or -1 for an unused slot; the used slots of a pair (q, p) come first; no partition mirrors its own masters; each master partition fills all 16 slots toward at least one partition.
All inputs are finite; a program needn't handle non-finite values.
Results may differ from the reference program's by a relative error of at most 0.0058.
Values may be sent and summed in bfloat16 or wider, within the bound.
A program may use at most 64 MiB of HBM per device.

```python
import jax
import jax.numpy as jnp
from jax import lax

D = 512
TILE = 128
MAST = 3072
SLOTS = 16
TILES = 72
VERT = 196608
NB = 32
N_DOM = 64


def draw_replica(key, part):
    base = jax.random.fold_in(key, 11)
    key_slots, key_used = jax.random.split(base, 2)
    slot_draw = jax.random.randint(key_slots, (N_DOM, N_DOM, SLOTS), 0, MAST)
    used_count = jax.random.randint(key_used, (N_DOM, N_DOM, 1), SLOTS // 4, SLOTS + 1)
    master_part = jnp.arange(N_DOM)[:, None, None]
    mirror_part = jnp.arange(N_DOM)[None, :, None]
    used_count = jnp.where(mirror_part == (master_part * 7 + 3) % N_DOM, SLOTS, used_count)
    used_count = jnp.where(mirror_part == master_part, 0, used_count)
    position = jnp.arange(SLOTS)[None, None, :]
    return jnp.where(position < used_count, slot_draw, -1).astype(jnp.int32)


def place_ends(values, own_key, low, high):
    dims = values.shape
    place = [jax.random.randint(jax.random.fold_in(own_key, axis), (), 0, dims[axis]) for axis in range(len(dims))]
    values = values.at[tuple(place)].set(low)
    longest = dims.index(max(dims))
    place[longest] = (place[longest] + 1) % dims[longest]
    return values.at[tuple(place)].set(high)


def strengthened(values, key, source, target, parts, factor):
    def block_of(dim):
        return (jnp.arange(values.shape[dim]) // (values.shape[dim] // parts)).reshape((-1,) + (1,) * (values.ndim - 1 - dim))

    one_side = jax.random.permutation(key, parts)[block_of(target)]
    far = (block_of(target) + parts // 2) % parts
    return jnp.where((block_of(source) == one_side) | (block_of(source) == far), factor * values, values)


def block_levels(own_key, shape, shards, smallest, largest):
    level, own = 1.0, jax.random.fold_in(own_key, 6)
    for dim, blocks in shards:
        heights = jnp.exp(jax.random.uniform(jax.random.fold_in(own, dim), (blocks,), jnp.float32, smallest / len(shards), largest / len(shards)))
        level = level * jnp.repeat(heights, shape[dim] // blocks).reshape([-1 if axis == dim else 1 for axis in range(len(shape))])
    return level


def scatter_about(own_key, shape, width, limit, pieces=(), kind=jnp.bfloat16):
    array = width * jax.random.normal(own_key, shape, jnp.float32)
    if pieces:
        array = array * block_levels(own_key, shape, pieces, -0.22, 0.18)
    return jnp.clip(array, -limit, limit).astype(kind)


def gaussian_with(rng, dims, width, reach, pieces, heavy, kind=jnp.bfloat16):
    array = width * jax.random.normal(rng, dims, jnp.float32)
    if pieces:
        array = array * block_levels(rng, dims, pieces, -0.22, 0.18)
    return jnp.clip(strengthened(array, jax.random.fold_in(rng, 3), *heavy), -reach, reach).astype(kind)


def setup_inputs(seed: int = 0) -> dict:
    keys = jax.random.split(jax.random.key(seed), 8)
    return {
        "features": gaussian_with(keys[0], (D, VERT), 1.0, 16.0, ((0, 8), (1, 64)), (1, 0, 64, 4.0)),
        "weights": scatter_about(keys[1], (2, D, D), (2 * D) ** -0.5, 0.1875),
        "tile_values": jnp.clip(0.099609375 * jax.random.uniform(keys[2], (N_DOM * TILES, TILE, TILE), jnp.float32) ** block_levels(keys[2], (N_DOM * TILES, TILE, TILE), ((0, 64),), -0.2, 0.2), 0.0, 0.099609375).astype(jnp.bfloat16),
        "tile_blocks": place_ends(jax.random.randint(keys[3], (N_DOM * TILES, 2), 0, NB), jax.random.fold_in(keys[3], 1), 0, NB - 1).astype(jnp.int32),
        "tile_counts": place_ends(jax.random.randint(keys[4], (N_DOM,), TILES // 2, TILES + 1), jax.random.fold_in(keys[4], 1), TILES // 2, TILES).astype(jnp.int32),
        "replica": draw_replica(jax.random.fold_in(keys[7], 71), 0),
        "cotangent": scatter_about(keys[6], (D, VERT), 1.0, 6.0, ((1, 512),)),
    }


def spread_field(values_in, tile_values, tile_blocks, tile_live, replica, forward):
    nblocks = (MAST + N_DOM * SLOTS) // TILE
    vertices = MAST * N_DOM
    edge_values = tile_values.reshape(N_DOM, TILES, TILE, TILE).astype(jnp.float32)
    block_pairs = tile_blocks.reshape(N_DOM, TILES, 2)
    feat_width = values_in.shape[0]

    def advance(summed, source):
        rows_here = replica[:, source, :]
        slot_used = (rows_here >= 0).reshape(-1)
        master_base = (jnp.arange(N_DOM, dtype=jnp.int32) * MAST)[:, None]
        global_cols = (master_base + jnp.where(rows_here >= 0, rows_here, 0)).reshape(-1).astype(jnp.int32)
        mirrors = jnp.where(slot_used[None, :], jnp.take(values_in, global_cols, axis=1), jnp.zeros((), values_in.dtype))
        own_cols = lax.dynamic_slice_in_dim(values_in, (source * MAST).astype(jnp.int32), MAST, 1)
        local_cols = jnp.concatenate([own_cols, mirrors], 1).astype(jnp.float32).reshape(feat_width, nblocks, TILE)
        source_blocks = block_pairs[source, :, 0]
        target_blocks = block_pairs[source, :, 1]
        if forward:
            picked = jnp.take(local_cols, source_blocks, axis=1)
            contrib = jnp.einsum('fts,tsd->ftd', picked, edge_values[source], precision=lax.Precision.HIGHEST)
            segment = target_blocks
        else:
            picked = jnp.take(local_cols, target_blocks, axis=1)
            contrib = jnp.einsum('ftd,tsd->fts', picked, edge_values[source], precision=lax.Precision.HIGHEST)
            segment = source_blocks
        contrib = contrib * tile_live[source][None, :, None]
        partial_value = jax.ops.segment_sum(jnp.moveaxis(contrib, 1, 0), segment, num_segments=nblocks)
        partial_value = jnp.moveaxis(partial_value, 0, 1).reshape(feat_width, nblocks * TILE)
        target_cols = jnp.concatenate([source * MAST + jnp.arange(MAST, dtype=jnp.int32),
                                       jnp.where(slot_used, global_cols, vertices).astype(jnp.int32)])
        summed = summed.at[:, target_cols].add(partial_value, mode="drop")
        return summed, None

    summed, _ = lax.scan(advance, jnp.zeros((feat_width, vertices), jnp.float32), jnp.arange(N_DOM, dtype=jnp.int32))
    return summed


def reference(features, weights, tile_values, tile_blocks, tile_counts, replica, cotangent):
    tile_live = (jnp.arange(TILES, dtype=jnp.int32)[None, :] < tile_counts[:, None]).astype(jnp.float32)
    aggregate = spread_field(features, tile_values, tile_blocks, tile_live, replica, True).astype(jnp.bfloat16)
    w_self = weights[0]
    w_neigh = weights[1]
    preact = jnp.dot(w_self.T, features, preferred_element_type=jnp.float32) + jnp.dot(w_neigh.T, aggregate, preferred_element_type=jnp.float32)
    sigmoid_z = jax.nn.sigmoid(preact)
    output = (preact * sigmoid_z).astype(jnp.bfloat16)
    slope = sigmoid_z * (1.0 + preact * (1.0 - sigmoid_z))
    pre_grad = (cotangent.astype(jnp.float32) * slope).astype(jnp.bfloat16)
    weight_grad = jnp.stack([jnp.dot(features, pre_grad.T, preferred_element_type=jnp.float32),
                             jnp.dot(aggregate, pre_grad.T, preferred_element_type=jnp.float32)])
    self_grad = jnp.dot(w_self, pre_grad, preferred_element_type=jnp.float32).astype(jnp.bfloat16)
    agg_grad = jnp.dot(w_neigh, pre_grad, preferred_element_type=jnp.float32).astype(jnp.bfloat16)
    back_terms = spread_field(agg_grad, tile_values, tile_blocks, tile_live, replica, False)
    feature_grad = (self_grad.astype(jnp.float32) + back_terms).astype(jnp.bfloat16)
    return (output, feature_grad, weight_grad)
```

```python
import functools

import jax
import jax.numpy as jnp
from jax import lax
from jax.experimental import pallas as pl
from jax.experimental.pallas import tpu as pltpu
from jax.sharding import PartitionSpec as P

F32 = jnp.float32
BF16 = jnp.bfloat16
TILE = 128
WIDTH = 64
HALF = 8
ROWS = 3 * TILE


def nn(a, b):
    return lax.dot_general(a, b, (((1,), (0,)), ((), ())), preferred_element_type=F32)


def nt(a, b):
    return lax.dot_general(a, b, (((1,), (1,)), ((), ())), preferred_element_type=F32)


def iota(shape, dim):
    return lax.broadcasted_iota(jnp.int32, shape, dim)


def clamp(i, n):
    return jnp.minimum(jnp.maximum(i, 0), n - 1)


def tile_order(seg, src, tiles):
    wide = (tiles, TILE)
    lane, row = iota(wide, 1), iota(wide, 0)
    eye = lane == row
    pad = lane < tiles
    number = iota((tiles, 1), 0)
    key = seg * tiles + number

    def as_row(col):
        return jnp.sum(jnp.where(eye, col, 0), axis=0, keepdims=True)

    rank = jnp.sum(jnp.where(pad & (as_row(key) < key), 1, 0), axis=1, keepdims=True)
    begin = jnp.sum(jnp.where(pad & (as_row(seg) < seg), 1, 0), axis=1, keepdims=True)
    perm = rank == lane

    def sort(col):
        return jnp.sum(jnp.where(perm, col, 0), axis=0, keepdims=True)

    goes_on = jnp.where(rank == begin, 0, 1)
    last = jnp.sum(jnp.where(seg <= lane, 1, 0), axis=0, keepdims=True) - 1
    some = jnp.minimum(jnp.sum(jnp.where(seg == lane, 1, 0), axis=0, keepdims=True), 1)
    return [sort(number), sort(src), sort(goes_on), jnp.maximum(last, 0), some]


def kernel(
    n_dom, nf,
    f_ref, w_ref, tile_ref, tb_ref, tc_ref, rep_ref, cot_ref,
    out_ref, fg_ref, wg_ref,
    loc, loc2, oh, seg, snd, rcv, xbuf, meta_v, meta_s, wt, rows2, asend, pre0, pgrad, gsend, ssend, sgr,
    wsend, wpair, wown, wzs, wz, wps, wq, wfin, wall,
    meta_sem, ssems, rsems,
):
    me, mf = lax.axis_index("dom"), lax.axis_index("feat")
    ny = n_dom // 8
    chips = n_dom // 2
    my_y, core, chip = me // 8, lax.rem(me, 2), me // 2
    tiles = tile_ref.shape[0]
    width = nf * WIDTH
    nmast = 3 * nf

    barrier = pltpu.get_barrier_semaphore()

    def greet_dom(i, _):
        pl.semaphore_signal(barrier, inc=1, device_id={"dom": lax.rem(me + i, n_dom)})
        return 0

    def greet_feat(i, _):
        pl.semaphore_signal(barrier, inc=1, device_id={"feat": lax.rem(mf + i, nf)})
        return 0

    lax.fori_loop(1, n_dom, greet_dom, 0)
    lax.fori_loop(1, nf, greet_feat, 0)

    def dom_copy(src, dst, sem, peer):
        return pltpu.make_async_remote_copy(src, dst, ssems.at[sem], rsems.at[sem], device_id={"dom": peer})

    def feat_copy(src, dst, sem, peer):
        return pltpu.make_async_remote_copy(src, dst, ssems.at[sem], rsems.at[sem], device_id={"feat": peer})

    some_dom, some_feat = lax.rem(me + 1, n_dom), lax.rem(mf + 1, nf)

    for b in range(nmast):
        loc[b] = f_ref[:, b * TILE : (b + 1) * TILE]

    def build(g, _):
        rep = jnp.concatenate(
            [jnp.broadcast_to(rep_ref[0, pl.ds(g * 8 + i, 1), :], (HALF, 16)) for i in range(8)], axis=0
        ).astype(F32)
        lane, sub = iota((64, 16), 1), iota((64, 16), 0) & 7
        cols = [
            jnp.sum(jnp.where(lane == sub + 8 * h, rep, 0.0), axis=1, keepdims=True) for h in range(2)
        ]
        diff = jnp.concatenate(cols, axis=0) - iota((TILE, TILE), 1).astype(F32)
        for b in range(nmast):
            oh[pl.ds(pl.multiple_of(g * TILE, TILE), TILE), b * TILE : (b + 1) * TILE] = jnp.where(
                diff == float(b * TILE), 1.0, 0.0
            ).astype(BF16)
        return 0

    lax.fori_loop(0, ny, build, 0)

    live = iota((tiles, 1), 0) < tc_ref[0]
    source, target = tb_ref[:, 0:1], tb_ref[:, 1:2]
    table = []
    for to, frm in ((target, source), (source, target)):
        table += tile_order(jnp.where(live, to, nmast + ny), frm, tiles)
    for r, line in enumerate(table):
        meta_v[r : r + 1, :] = line
    meta_copy = pltpu.make_async_copy(meta_v, meta_s, meta_sem)
    meta_copy.start()

    r_i, c_i = iota((TILE, TILE), 0), iota((TILE, TILE), 1)
    place = ((r_i >> 3) & 7) * 16 + (r_i >> 6) * 8 + (r_i & 7)
    perm = jnp.where(place == c_i, 1.0, 0.0).astype(BF16)

    def own_zero(x):
        for d in (0, 1):
            rcv[2 * x + d, pl.ds(me, 1)] = jnp.zeros((1, HALF, TILE), BF16)

    own_zero(0)
    own_zero(1)

    pl.semaphore_wait(barrier, n_dom - 1 + nf - 1)

    def send_group(x, g, packed):
        snd[x, pl.ds(g * 8, 8)] = packed.reshape(8, HALF, TILE).astype(BF16)

        def one(i, _):
            p = g * 8 + i

            @pl.when(p != me)
            def _():
                dom_copy(snd.at[x, p], rcv.at[x, me], x, p).start()

            return 0

        lax.fori_loop(0, 8, one, 0)

    def pull(x, values):
        def body(s, _):
            g = lax.rem(my_y + s, ny)
            field = jnp.concatenate([values[b] for b in range(nmast)], axis=1)
            o = nt(oh[pl.ds(pl.multiple_of(g * TILE, TILE), TILE), :], field)
            send_group(x, g, jnp.concatenate([o[:64], o[64:]], axis=1))
            return 0

        lax.fori_loop(1, ny + 1, body, 0)

    def await_dom(x):
        dom_copy(snd.at[x, pl.ds(0, n_dom - 1)], rcv.at[x, pl.ds(0, n_dom - 1)], x, some_dom).wait_recv()

    def unpacked(x, g):
        r = rcv[x, pl.ds(g * 8, 8)].astype(F32).reshape(64, TILE)
        t = jnp.transpose(r)
        return jnp.concatenate([t[:64], t[64:]], axis=1).astype(BF16)

    def mirrors_in(x, values):
        def body(g, _):
            values[nmast + g] = nn(unpacked(x, g), perm).astype(BF16)
            return 0

        lax.fori_loop(0, ny, body, 0)

    def multiply(values, base, forward):
        def body(j, run):
            lhs = values[clamp(meta_s[base + 1, j], nmast + ny)]
            mat = tile_ref[clamp(meta_s[base, j], tiles)]
            contrib = nn(lhs, mat) if forward else nt(lhs, mat)
            run = run * meta_s[base + 2, j].astype(F32) + contrib
            seg[j] = run
            return run

        lax.fori_loop(0, tiles, body, jnp.zeros((WIDTH, TILE), F32), unroll=8)

    def partial(base, c):
        return seg[clamp(meta_s[base + 3, c], tiles)] * meta_s[base + 4, c].astype(F32)

    def push(x, base):
        def body(s, _):
            g = lax.rem(my_y + s, ny)
            o = nt(perm, partial(base, nmast + g).astype(BF16))
            send_group(x, g, jnp.concatenate([o[:64], o[64:]], axis=1))
            return 0

        lax.fori_loop(1, ny + 1, body, 0)

    def mirrors_back(x):
        def body(g, _):
            xbuf[:, pl.ds(pl.multiple_of(g * TILE, TILE), TILE)] = unpacked(x, g)
            return 0

        lax.fori_loop(0, ny, body, 0)

    def summed(base, j):
        own = jnp.concatenate([partial(base, 3 * j + r) for r in range(3)], axis=1)
        return own + nn(xbuf[...], oh[:, pl.ds(pl.multiple_of(j * ROWS, TILE), ROWS)])

    my_rows = pl.ds(pl.multiple_of(mf * WIDTH, WIDTH), WIDTH)
    S_F, S_A, S_G, S_S, S_W, S_Z, S_Q, S_L = range(4, 12)

    pull(0, loc)

    def send_features(s, _):
        j = lax.rem(mf + s, nf)
        feat_copy(
            f_ref.at[:, pl.ds(pl.multiple_of(j * ROWS, TILE), ROWS)], rows2.at[0, my_rows], S_F, j
        ).start()
        return 0

    lax.fori_loop(1, nf, send_features, 0)
    rows2[0, my_rows, :] = f_ref[:, pl.ds(pl.multiple_of(mf * ROWS, TILE), ROWS)]

    for k in range(2):
        for a in range(0, width, TILE):
            for b in range(0, width, TILE):
                wt[k, b : b + TILE, a : a + TILE] = jnp.transpose(
                    w_ref[k, a : a + TILE, b : b + TILE].astype(F32)
                ).astype(BF16)

    await_dom(0)
    mirrors_in(0, loc)
    meta_copy.wait()
    multiply(loc, 0, True)
    push(1, 0)

    def await_feat(buf, sem, peers=nf - 1):
        feat_copy(buf.at[pl.ds(0, peers)], buf.at[pl.ds(0, peers)], sem, some_feat).wait_recv()

    def await_rows(k, sem):
        got = rows2.at[k, pl.ds(0, (nf - 1) * WIDTH)]
        feat_copy(got, got, sem, some_feat).wait_recv()

    await_rows(0, S_F)

    def own_half(c, _):
        at = pl.ds(pl.multiple_of(c * TILE, TILE), TILE)
        pre0[at, :] = nn(wt[0, at, :], rows2[0])
        return 0

    lax.fori_loop(0, width // TILE, own_half, 0)

    await_dom(1)
    mirrors_back(1)

    def send_aggregate(s, _):
        j = lax.rem(mf + s, nf)
        asend[j] = summed(0, j).astype(BF16)

        @pl.when(j != mf)
        def _():
            feat_copy(asend.at[j], rows2.at[1, my_rows], S_A, j).start()

        @pl.when(j == mf)
        def _():
            rows2[1, my_rows, :] = asend[j]

        return 0

    lax.fori_loop(1, nf + 1, send_aggregate, 0)
    await_rows(1, S_A)

    def dense(c, _):
        at = pl.ds(pl.multiple_of(c * TILE, TILE), TILE)
        z = pre0[at, :] + nn(wt[1, at, :], rows2[1])
        s = jax.nn.sigmoid(z)
        out_ref[at, :] = (z * s).astype(BF16)
        slope = s * (1.0 + z * (1.0 - s))
        pgrad[at, :] = (cot_ref[at, :].astype(F32) * slope).astype(BF16)
        return 0

    lax.fori_loop(0, width // TILE, dense, 0)

    def blocked(v):
        return [v[:, r * TILE : (r + 1) * TILE].astype(BF16) for r in range(3)]

    def send_agg_grad(s, _):
        j = lax.rem(mf + s, nf)
        v = nn(w_ref[1, pl.ds(pl.multiple_of(j * WIDTH, WIDTH), WIDTH), :], pgrad[...])
        for r, part in enumerate(blocked(v)):
            gsend[j, r] = part

        @pl.when(j != mf)
        def _():
            feat_copy(gsend.at[j], loc2.at[pl.ds(3 * mf, 3)], S_G, j).start()

        @pl.when(j == mf)
        def _():
            for r in range(3):
                loc2[3 * mf + r] = gsend[j, r]

        return 0

    lax.fori_loop(1, nf + 1, send_agg_grad, 0)

    mate = me + 1 - 2 * core

    def other_terms(c, _):
        at = pl.ds(pl.multiple_of(c * TILE, TILE), TILE)
        wsend[at, :] = nt(rows2[1 - core, at, :], pgrad[...]).astype(BF16)
        return 0

    lax.fori_loop(0, width // TILE, other_terms, 0)
    dom_copy(wsend, wpair, S_W, mate).start()

    def send_self_grad(s, _):
        j = lax.rem(mf + s, nf)
        ssend[j] = nn(w_ref[0, pl.ds(pl.multiple_of(j * WIDTH, WIDTH), WIDTH), :], pgrad[...]).astype(BF16)

        @pl.when(j != mf)
        def _():
            feat_copy(ssend.at[j], sgr.at[mf], S_S, j).start()

        @pl.when(j == mf)
        def _():
            sgr[mf] = ssend[j]

        return 0

    lax.fori_loop(1, nf + 1, send_self_grad, 0)

    def own_terms(c, _):
        at = pl.ds(pl.multiple_of(c * TILE, TILE), TILE)
        wown[at, :] = nt(rows2[core, at, :], pgrad[...])
        return 0

    lax.fori_loop(0, width // TILE, own_terms, 0)

    got = loc2.at[pl.ds(0, 3 * (nf - 1))]
    feat_copy(got, got, S_G, some_feat).wait_recv()
    pull(2, loc2)

    dom_copy(wsend, wpair, S_W, mate).wait_recv()

    def send_terms(s, _):
        j = lax.rem(mf + s, nf)
        at = pl.ds(pl.multiple_of(j * WIDTH, WIDTH), WIDTH)
        wzs[j] = (wown[at, :] + wpair[at, :].astype(F32)).astype(BF16)

        @pl.when(j != mf)
        def _():
            feat_copy(wzs.at[j], wz.at[mf], S_Z, j).start()

        @pl.when(j == mf)
        def _():
            wz[mf] = wzs[j]

        return 0

    lax.fori_loop(1, nf + 1, send_terms, 0)

    await_dom(2)
    mirrors_in(2, loc2)
    multiply(loc2, 5, False)
    push(3, 5)

    await_feat(wz, S_Z)
    pr, pc = WIDTH // ny, width // 4
    total = wz[0].astype(F32)
    for j in range(1, nf):
        total = total + wz[j].astype(F32)
    for y in range(ny):
        for x in range(4):
            wps[4 * y + x] = total[y * pr : (y + 1) * pr, x * pc : (x + 1) * pc].astype(BF16)

    def send_pieces(i, _):
        p = lax.rem(chip + i, chips)
        dom_copy(wps.at[p], wq.at[chip], S_Q, 2 * p + core).start()
        return 0

    lax.fori_loop(1, chips, send_pieces, 0)
    wq[chip] = wps[chip]

    await_feat(sgr, S_S)
    await_dom(3)
    mirrors_back(3)

    def finish(j, _):
        at = pl.ds(pl.multiple_of(j * ROWS, TILE), ROWS)
        fg_ref[:, at] = (sgr[j].astype(F32) + summed(5, j)).astype(BF16)
        return 0

    dom_copy(wq.at[pl.ds(0, chips - 1)], wq.at[pl.ds(0, chips - 1)], S_Q, some_dom).wait_recv()
    whole = wq[0].astype(F32)
    for i in range(1, chips):
        whole = whole + wq[i].astype(F32)
    wfin[...] = whole.astype(BF16)
    wall[me] = whole.astype(BF16)

    def send_final(i, _):
        dom_copy(wfin, wall.at[me], S_L, lax.rem(me + i, n_dom)).start()
        return 0

    lax.fori_loop(1, n_dom, send_final, 0)

    lax.fori_loop(0, nf, finish, 0)

    dom_copy(wall.at[pl.ds(0, n_dom - 1)], wall.at[pl.ds(0, n_dom - 1)], S_L, some_dom).wait_recv()
    for d in range(n_dom):
        y, x, c = d // 8, (d // 2) % 4, d % 2
        wg_ref[c, y * pr : (y + 1) * pr, x * pc : (x + 1) * pc] = wall[d].astype(F32)

    for x in range(4):
        dom_copy(snd.at[x, pl.ds(0, n_dom - 1)], rcv.at[x, pl.ds(0, n_dom - 1)], x, some_dom).wait_send()
    for sem, buf in ((S_F, asend), (S_A, asend), (S_G, gsend), (S_S, ssend), (S_Z, wzs)):
        part = buf.at[pl.ds(0, nf - 1)]
        feat_copy(part, part, sem, some_feat).wait_send()
    dom_copy(wsend, wpair, S_W, mate).wait_send()
    dom_copy(wps.at[pl.ds(0, chips - 1)], wq.at[pl.ds(0, chips - 1)], S_Q, some_dom).wait_send()
    dom_copy(wall.at[pl.ds(0, n_dom - 1)], wall.at[pl.ds(0, n_dom - 1)], S_L, some_dom).wait_send()


def local(n_dom, nf, features, weights, tile_values, tile_blocks, tile_counts, replica, cotangent):
    width, tiles = nf * WIDTH, tile_values.shape[0]
    masters = features.shape[1]
    ny, chips = n_dom // 8, n_dom // 2
    nb = 3 * nf + ny
    piece = (WIDTH // ny, width // 4)
    vmem = pl.BlockSpec(memory_space=pltpu.VMEM)
    return pl.pallas_call(
        functools.partial(kernel, n_dom, nf),
        out_shape=(
            jax.ShapeDtypeStruct((width, ROWS), BF16),
            jax.ShapeDtypeStruct((WIDTH, masters), BF16),
            jax.ShapeDtypeStruct((2, WIDTH, width), F32),
        ),
        in_specs=[vmem, vmem, vmem, vmem, pl.BlockSpec(memory_space=pltpu.SMEM), vmem, vmem],
        out_specs=(vmem, vmem, vmem),
        scratch_shapes=[
            pltpu.VMEM((nb, WIDTH, TILE), BF16),
            pltpu.VMEM((nb, WIDTH, TILE), BF16),
            pltpu.VMEM((n_dom * 16, masters), BF16),
            pltpu.VMEM((tiles, WIDTH, TILE), F32),
            pltpu.VMEM((4, n_dom, HALF, TILE), BF16),
            pltpu.VMEM((4, n_dom, HALF, TILE), BF16),
            pltpu.VMEM((WIDTH, n_dom * 16), BF16),
            pltpu.VMEM((16, TILE), jnp.int32),
            pltpu.SMEM((16, TILE), jnp.int32),
            pltpu.VMEM((2, width, width), BF16),
            pltpu.VMEM((2, width, ROWS), BF16),
            pltpu.VMEM((nf, WIDTH, ROWS), BF16),
            pltpu.VMEM((width, ROWS), F32),
            pltpu.VMEM((width, ROWS), BF16),
            pltpu.VMEM((nf, 3, WIDTH, TILE), BF16),
            pltpu.VMEM((nf, WIDTH, ROWS), BF16),
            pltpu.VMEM((nf, WIDTH, ROWS), BF16),
            pltpu.VMEM((width, width), BF16),
            pltpu.VMEM((width, width), BF16),
            pltpu.VMEM((width, width), F32),
            pltpu.VMEM((nf, WIDTH, width), BF16),
            pltpu.VMEM((nf, WIDTH, width), BF16),
            pltpu.VMEM((chips, *piece), BF16),
            pltpu.VMEM((chips, *piece), BF16),
            pltpu.VMEM(piece, BF16),
            pltpu.VMEM((n_dom, *piece), BF16),
            pltpu.SemaphoreType.DMA,
            pltpu.SemaphoreType.DMA((12,)),
            pltpu.SemaphoreType.DMA((12,)),
        ],
        compiler_params=pltpu.CompilerParams(
            collective_id=0, has_side_effects=True, vmem_limit_bytes=48 * 2**20
        ),
    )(features, weights, tile_values, tile_blocks, tile_counts, replica, cotangent)


def solution(mesh):
    return jax.shard_map(
        functools.partial(local, mesh.shape["dom"], mesh.shape["feat"]),
        mesh=mesh,
        in_specs=(
            P("feat", "dom"),
            P(),
            P("dom", None, None),
            P("dom", None),
            P("dom"),
            P("dom", None, None),
            P(None, ("dom", "feat")),
        ),
        out_specs=(P(None, ("dom", "feat")), P("feat", "dom"), P(None, "feat", None)),
        check_vma=False,
    )
```

```python
import functools

import jax
import jax.numpy as jnp
from jax import lax
from jax.experimental import pallas as pl
from jax.experimental.pallas import tpu as pltpu
from jax.sharding import PartitionSpec as P

F32 = jnp.float32
BF16 = jnp.bfloat16
TILE = 128
WIDTH = 64
HALF = 8
ROWS = 3 * TILE


def nn(a, b):
    return lax.dot_general(a, b, (((1,), (0,)), ((), ())), preferred_element_type=F32)


def nt(a, b):
    return lax.dot_general(a, b, (((1,), (1,)), ((), ())), preferred_element_type=F32)


def iota(shape, dim):
    return lax.broadcasted_iota(jnp.int32, shape, dim)


def clamp(i, n):
    return jnp.minimum(jnp.maximum(i, 0), n - 1)


def tile_order(seg, src, tiles):
    lane, row = iota((tiles, TILE), 1), iota((tiles, TILE), 0)
    eye = iota((tiles, tiles), 0) == iota((tiles, tiles), 1)
    number = iota((1, tiles), 1)

    def as_col(line):
        return jnp.sum(jnp.where(eye, line, 0), axis=1, keepdims=True)

    key = seg * tiles + number
    seg_col, key_col = as_col(seg), as_col(key)
    rank = jnp.sum(jnp.where(key < key_col, 1, 0), axis=1, keepdims=True)
    begin = jnp.sum(jnp.where(seg < seg_col, 1, 0), axis=1, keepdims=True)
    perm = rank == lane

    def sort(col):
        return jnp.sum(jnp.where(perm, col, 0), axis=0, keepdims=True)

    goes_on = jnp.where(rank == begin, 0, 1)
    last = jnp.sum(jnp.where(seg_col <= lane, 1, 0), axis=0, keepdims=True) - 1
    some = jnp.minimum(jnp.sum(jnp.where(seg_col == lane, 1, 0), axis=0, keepdims=True), 1)
    return [sort(row[:, 0:1]), sort(as_col(src)), sort(goes_on), jnp.maximum(last, 0), some]


def kernel(
    n_dom, nf,
    f_in, w_in, tile_in, tb_in, tc_ref, rep_in, cot_in,
    out_ref, fg_ref, wg_ref,
    f_ref, w_ref, tile_ref, tb_ref, rep_ref, cot_ref,
    loc, loc2, oh, seg, snd, rcv, xbuf, acc, meta_v, meta_s, wt, rows, asend, pre0, pgrad, gsend, ssend, sgr,
    wsend, wpair, wown, wzs, wz, wps, wq, wfin, wall,
    meta_sem, load_sems, ssems, rsems,
):
    me, mf = lax.axis_index("dom"), lax.axis_index("feat")
    ny = n_dom // 8
    chips = n_dom // 2
    my_y, core, chip = me // 8, lax.rem(me, 2), me // 2
    tiles = tile_in.shape[0]
    width = nf * WIDTH
    nmast = 3 * nf
    span = nf * TILE

    loads = [
        pltpu.make_async_copy(src, dst, load_sems.at[i])
        for i, (src, dst) in enumerate(
            (
                (rep_in, rep_ref),
                (f_in, f_ref),
                (tb_in, tb_ref),
                (w_in, w_ref),
                (tile_in, tile_ref),
                (cot_in, cot_ref),
            )
        )
    ]
    for load in loads:
        load.start()

    barrier = pltpu.get_barrier_semaphore()

    def greet_dom(i, _):
        pl.semaphore_signal(barrier, inc=1, device_id={"dom": lax.rem(me + i, n_dom)})
        return 0

    def greet_feat(i, _):
        pl.semaphore_signal(barrier, inc=1, device_id={"feat": lax.rem(mf + i, nf)})
        return 0

    lax.fori_loop(1, n_dom, greet_dom, 0)
    lax.fori_loop(1, nf, greet_feat, 0)

    def dom_copy(src, dst, sem, peer):
        return pltpu.make_async_remote_copy(src, dst, ssems.at[sem], rsems.at[sem], device_id={"dom": peer})

    def feat_copy(src, dst, sem, peer):
        return pltpu.make_async_remote_copy(src, dst, ssems.at[sem], rsems.at[sem], device_id={"feat": peer})

    some_dom, some_feat = lax.rem(me + 1, n_dom), lax.rem(mf + 1, nf)
    my_rows = pl.ds(pl.multiple_of(mf * WIDTH, WIDTH), WIDTH)
    S_F, S_A, S_G, S_S, S_W, S_Z, S_Q, S_L = 4, 5, 8, 11, 12, 13, 14, 15

    def far_first(start, n, step):
        def body(s, _):
            away = n // 2 + ((s + 1) // 2) * (1 - 2 * lax.rem(s, 2))
            step(lax.rem(start + away, n))
            return 0

        lax.fori_loop(0, n, body, 0)

    def rows_of(c):
        return pl.ds(pl.multiple_of(c * TILE, TILE), TILE)

    loads[0].wait()
    loads[1].wait()
    for b in range(nmast):
        loc[b] = f_ref[:, b * TILE : (b + 1) * TILE]

    def build(g, _):
        wide = (8 * HALF, n_dom)
        mine = iota(wide, 1) == g * 8 + (iota(wide, 0) >> 3)
        cols = []
        for h in range(2):
            slots = rep_ref[0, h * HALF : (h + 1) * HALF, :].astype(F32)
            slots = jnp.concatenate([slots] * 8, axis=0)
            cols.append(jnp.sum(jnp.where(mine, slots, 0.0), axis=1, keepdims=True))
        diff = jnp.concatenate(cols, axis=0) - iota((TILE, TILE), 1).astype(F32)
        for r in range(3):
            for f in range(nf):
                at = r * span + f * TILE
                oh[rows_of(g), at : at + TILE] = jnp.where(
                    diff == float((3 * f + r) * TILE), 1.0, 0.0
                ).astype(BF16)
        return 0

    lax.fori_loop(0, ny, build, 0)

    for x in range(4):
        rcv[x, pl.ds(me, 1)] = jnp.zeros((1, HALF, TILE), BF16)

    def chunk(values, r):
        return jnp.concatenate([values[3 * f + r] for f in range(nf)], axis=1)

    def pack(x, g, o):
        side_by_side = jnp.concatenate([o[:64], o[64:]], axis=1)
        snd[x, pl.ds(g * 8, 8)] = side_by_side.reshape(8, HALF, TILE).astype(BF16)

    def send_group(x, g):
        def one(i, _):
            p = g * 8 + i

            @pl.when(p != me)
            def _():
                dom_copy(snd.at[x, p], rcv.at[x, me], x, p).start()

            return 0

        lax.fori_loop(0, 8, one, 0)

    def first_pull(g, _):
        field = jnp.concatenate([chunk(loc, r) for r in range(3)], axis=1)
        pack(0, g, nt(oh[rows_of(g), :], field))
        return 0

    lax.fori_loop(0, ny, first_pull, 0)

    loads[2].wait()
    live = iota((1, tiles), 1) < tc_ref[0]
    source, target = tb_ref[0:1, :], tb_ref[1:2, :]
    table = []
    for to, frm in ((target, source), (source, target)):
        table += tile_order(jnp.where(live, to, nmast + ny), frm, tiles)
    for r, line in enumerate(table):
        meta_v[r : r + 1, :] = line
    meta_copy = pltpu.make_async_copy(meta_v, meta_s, meta_sem)
    meta_copy.start()

    r_i, c_i = iota((TILE, TILE), 0), iota((TILE, TILE), 1)
    place = ((r_i >> 3) & 7) * 16 + (r_i >> 6) * 8 + (r_i & 7)
    perm = jnp.where(place == c_i, 1.0, 0.0).astype(BF16)

    loads[3].wait()
    for k in range(2):
        for a in range(0, width, TILE):
            for b in range(0, width, TILE):
                wt[k, b : b + TILE, a : a + TILE] = jnp.transpose(
                    w_ref[k, a : a + TILE, b : b + TILE].astype(F32)
                ).astype(BF16)
    loads[4].wait()
    loads[5].wait()
    meta_copy.wait()

    pl.semaphore_wait(barrier, n_dom - 1 + nf - 1)

    far_first(my_y, ny, lambda g: send_group(0, g))

    def send_features(j):
        theirs = loc.at[pl.ds(3 * j, 3)]

        @pl.when(j != mf)
        def _():
            feat_copy(theirs, rows.at[0, :, my_rows, :], S_F, j).start()

    far_first(mf, nf, send_features)
    for r in range(3):
        rows[0, r, my_rows, :] = loc[3 * mf + r]

    def await_dom(x):
        dom_copy(snd.at[x, pl.ds(0, n_dom - 1)], rcv.at[x, pl.ds(0, n_dom - 1)], x, some_dom).wait_recv()

    def await_blocks(buf, sem, n):
        feat_copy(buf.at[pl.ds(0, n)], buf.at[pl.ds(0, n)], sem, some_feat).wait_recv()

    def unpacked(x, g):
        t = jnp.transpose(rcv[x, pl.ds(g * 8, 8)].astype(F32).reshape(64, TILE))
        return jnp.concatenate([t[:64], t[64:]], axis=1).astype(BF16)

    def mirrors_in(x, values):
        def body(g, _):
            values[nmast + g] = nn(unpacked(x, g), perm).astype(BF16)
            return 0

        lax.fori_loop(0, ny, body, 0)

    def multiply(values, base, forward, low, high, start):
        def body(j, run):
            lhs = values[clamp(meta_s[base + 1, j], nmast + ny)]
            mat = tile_ref[clamp(meta_s[base, j], tiles)]
            contrib = nn(lhs, mat) if forward else nt(lhs, mat)
            run = run * meta_s[base + 2, j].astype(F32) + contrib
            seg[j] = run
            return run

        return lax.fori_loop(low, high, body, start, unroll=12)

    def partial(base, c):
        return seg[clamp(meta_s[base + 3, c], tiles)] * meta_s[base + 4, c].astype(F32)

    def push(x, base):
        def body(g):
            pack(x, g, nt(perm, partial(base, nmast + g).astype(BF16)))
            send_group(x, g)

        far_first(my_y, ny, body)

    def mirrors_back(x):
        def body(g, _):
            xbuf[:, rows_of(g)] = unpacked(x, g)
            return 0

        lax.fori_loop(0, ny, body, 0)

    def summed(base, j, r):
        at = pl.ds(pl.multiple_of(r * span + j * TILE, TILE), TILE)
        return partial(base, 3 * j + r) + nn(xbuf[...], oh[:, at])

    nothing = jnp.zeros((WIDTH, TILE), F32)
    await_dom(0)
    mirrors_in(0, loc)
    multiply(loc, 0, True, 0, tiles, nothing)
    push(1, 0)

    await_blocks(loc, S_F, 3 * (nf - 1))

    def own_half(c, _):
        for r in range(3):
            pre0[r, rows_of(c), :] = nn(wt[0, rows_of(c), :], rows[0, r])
        return 0

    lax.fori_loop(0, width // TILE, own_half, 0)

    await_dom(1)
    mirrors_back(1)

    for r in range(3):

        def send_aggregate(j, r=r):
            asend[r, j] = summed(0, j, r).astype(BF16)

            @pl.when(j != mf)
            def _():
                feat_copy(asend.at[r, j], rows.at[1, r, my_rows, :], S_A + r, j).start()

            @pl.when(j == mf)
            def _():
                rows[1, r, my_rows, :] = asend[r, j]

        far_first(mf, nf, send_aggregate)

    for r in range(3):
        await_blocks(asend.at[r], S_A + r, nf - 1)

        def dense(c, _, r=r):
            at = rows_of(c)
            z = pre0[r, at, :] + nn(wt[1, at, :], rows[1, r])
            s = jax.nn.sigmoid(z)
            out_ref[at, r * TILE : (r + 1) * TILE] = (z * s).astype(BF16)
            slope = s * (1.0 + z * (1.0 - s))
            cot = cot_ref[at, r * TILE : (r + 1) * TILE].astype(F32)
            pgrad[r, at, :] = (cot * slope).astype(BF16)
            return 0

        lax.fori_loop(0, width // TILE, dense, 0)

        def agg_grad(c, _, r=r):
            v = nn(w_ref[1, rows_of(c), :], pgrad[r]).astype(BF16)
            gsend[r, 2 * c] = v[:WIDTH]
            gsend[r, 2 * c + 1] = v[WIDTH:]
            return 0

        lax.fori_loop(0, width // TILE, agg_grad, 0)

        def send_agg_grad(j, r=r):
            @pl.when(j != mf)
            def _():
                feat_copy(gsend.at[r, j], loc2.at[3 * mf + r], S_G + r, j).start()

            @pl.when(j == mf)
            def _():
                loc2[3 * mf + r] = gsend[r, j]

        far_first(mf, nf, send_agg_grad)

    mate = me + 1 - 2 * core

    def terms(k, c):
        mine = jnp.concatenate([rows[k, r, rows_of(c), :] for r in range(3)], axis=1)
        return nt(mine, jnp.concatenate([pgrad[r] for r in range(3)], axis=1))

    def other_terms(c, _):
        wsend[rows_of(c), :] = terms(1 - core, c).astype(BF16)
        return 0

    lax.fori_loop(0, width // TILE, other_terms, 0)
    dom_copy(wsend, wpair, S_W, mate).start()

    def own_terms(c, _):
        wown[rows_of(c), :] = terms(core, c)
        return 0

    lax.fori_loop(0, width // TILE, own_terms, 0)

    def gathered(g, r):
        return nt(oh[rows_of(g), r * span : (r + 1) * span], chunk(loc2, r))

    def pull_first(g, _):
        acc[g] = gathered(g, 0)
        return 0

    def pull_second(g, _):
        acc[g] = acc[g] + gathered(g, 1)
        return 0

    def pull_last(g):
        pack(2, g, acc[g] + gathered(g, 2))
        send_group(2, g)

    await_blocks(loc2, S_G, nf - 1)
    lax.fori_loop(0, ny, pull_first, 0)

    dom_copy(wsend, wpair, S_W, mate).wait_recv()

    def send_terms(j):
        at = pl.ds(pl.multiple_of(j * WIDTH, WIDTH), WIDTH)
        wzs[j] = (wown[at, :] + wpair[at, :].astype(F32)).astype(BF16)

        @pl.when(j != mf)
        def _():
            feat_copy(wzs.at[j], wz.at[mf], S_Z, j).start()

        @pl.when(j == mf)
        def _():
            wz[mf] = wzs[j]

    far_first(mf, nf, send_terms)

    await_blocks(loc2, S_G + 1, nf - 1)
    lax.fori_loop(0, ny, pull_second, 0)
    await_blocks(loc2, S_G + 2, nf - 1)
    far_first(my_y, ny, pull_last)

    def send_self_grad(j):
        w = w_ref[0, pl.ds(pl.multiple_of(j * WIDTH, WIDTH), WIDTH), :]
        for r in range(3):
            ssend[j, r] = nn(w, pgrad[r]).astype(BF16)

        @pl.when(j != mf)
        def _():
            feat_copy(ssend.at[j], sgr.at[mf], S_S, j).start()

        @pl.when(j == mf)
        def _():
            sgr[mf] = ssend[j]

    far_first(mf, nf, send_self_grad)

    await_dom(2)
    mirrors_in(2, loc2)
    run = multiply(loc2, 5, False, 0, tiles // 2, nothing)

    await_blocks(wz, S_Z, nf - 1)
    pr, pc = WIDTH // ny, width // 4
    total = wz[0].astype(F32)
    for j in range(1, nf):
        total = total + wz[j].astype(F32)
    for y in range(ny):
        for x in range(4):
            wps[4 * y + x] = total[y * pr : (y + 1) * pr, x * pc : (x + 1) * pc].astype(BF16)

    def send_pieces(i, _):
        p = lax.rem(chip + i, chips)
        dom_copy(wps.at[p], wq.at[chip], S_Q, 2 * p + core).start()
        return 0

    lax.fori_loop(1, chips, send_pieces, 0)
    wq[chip] = wps[chip]

    multiply(loc2, 5, False, tiles // 2, tiles, run)
    push(3, 5)

    dom_copy(wq.at[pl.ds(0, chips - 1)], wq.at[pl.ds(0, chips - 1)], S_Q, some_dom).wait_recv()
    whole = wq[0].astype(F32)
    for i in range(1, chips):
        whole = whole + wq[i].astype(F32)
    wfin[...] = whole.astype(BF16)
    wall[me] = whole.astype(BF16)

    def send_final(i, _):
        dom_copy(wfin, wall.at[me], S_L, lax.rem(me + i, n_dom)).start()
        return 0

    lax.fori_loop(1, n_dom, send_final, 0)

    await_blocks(sgr, S_S, nf - 1)
    await_dom(3)
    mirrors_back(3)

    def finish(j, _):
        for r in range(3):
            at = pl.ds(pl.multiple_of(j * ROWS + r * TILE, TILE), TILE)
            fg_ref[:, at] = (sgr[j, r].astype(F32) + summed(5, j, r)).astype(BF16)
        return 0

    lax.fori_loop(0, nf, finish, 0)

    dom_copy(wall.at[pl.ds(0, n_dom - 1)], wall.at[pl.ds(0, n_dom - 1)], S_L, some_dom).wait_recv()
    for d in range(n_dom):
        y, x, c = d // 8, (d // 2) % 4, d % 2
        wg_ref[c, y * pr : (y + 1) * pr, x * pc : (x + 1) * pc] = wall[d].astype(F32)

    for x in range(4):
        dom_copy(snd.at[x, pl.ds(0, n_dom - 1)], rcv.at[x, pl.ds(0, n_dom - 1)], x, some_dom).wait_send()

    def drain(buf, sem):
        part = buf.at[pl.ds(0, nf - 1)]
        feat_copy(part, part, sem, some_feat).wait_send()

    for sem, buf in ((S_F, ssend), (S_S, ssend), (S_Z, wzs)):
        drain(buf, sem)
    for r in range(3):
        drain(asend.at[r], S_A + r)
        drain(gsend.at[r], S_G + r)
    dom_copy(wsend, wpair, S_W, mate).wait_send()
    dom_copy(wps.at[pl.ds(0, chips - 1)], wq.at[pl.ds(0, chips - 1)], S_Q, some_dom).wait_send()
    dom_copy(wall.at[pl.ds(0, n_dom - 1)], wall.at[pl.ds(0, n_dom - 1)], S_L, some_dom).wait_send()


def pinned(x):
    return pltpu.with_memory_space_constraint(x, pltpu.HBM)


def local(n_dom, nf, features, weights, tile_values, tile_blocks, tile_counts, replica, cotangent):
    width, tiles = nf * WIDTH, tile_values.shape[0]
    masters = features.shape[1]
    ny, chips = n_dom // 8, n_dom // 2
    nb = 3 * nf + ny
    piece = (WIDTH // ny, width // 4)
    vmem = pl.BlockSpec(memory_space=pltpu.VMEM)
    hbm = pl.BlockSpec(memory_space=pltpu.HBM)
    return pl.pallas_call(
        functools.partial(kernel, n_dom, nf),
        out_shape=(
            jax.ShapeDtypeStruct((width, ROWS), BF16),
            jax.ShapeDtypeStruct((WIDTH, masters), BF16),
            jax.ShapeDtypeStruct((2, WIDTH, width), F32),
        ),
        in_specs=[hbm, hbm, hbm, hbm, pl.BlockSpec(memory_space=pltpu.SMEM), hbm, hbm],
        out_specs=(vmem, vmem, vmem),
        scratch_shapes=[
            pltpu.VMEM((WIDTH, masters), BF16),
            pltpu.VMEM((2, width, width), BF16),
            pltpu.VMEM((tiles, TILE, TILE), BF16),
            pltpu.VMEM((2, tiles), jnp.int32),
            pltpu.VMEM((1, 16, n_dom), jnp.int32),
            pltpu.VMEM((width, ROWS), BF16),
            pltpu.VMEM((nb, WIDTH, TILE), BF16),
            pltpu.VMEM((nb, WIDTH, TILE), BF16),
            pltpu.VMEM((n_dom * 16, masters), BF16),
            pltpu.VMEM((tiles, WIDTH, TILE), F32),
            pltpu.VMEM((4, n_dom, HALF, TILE), BF16),
            pltpu.VMEM((4, n_dom, HALF, TILE), BF16),
            pltpu.VMEM((WIDTH, n_dom * 16), BF16),
            pltpu.VMEM((ny, TILE, WIDTH), F32),
            pltpu.VMEM((16, TILE), jnp.int32),
            pltpu.SMEM((16, TILE), jnp.int32),
            pltpu.VMEM((2, width, width), BF16),
            pltpu.VMEM((2, 3, width, TILE), BF16),
            pltpu.VMEM((3, nf, WIDTH, TILE), BF16),
            pltpu.VMEM((3, width, TILE), F32),
            pltpu.VMEM((3, width, TILE), BF16),
            pltpu.VMEM((3, nf, WIDTH, TILE), BF16),
            pltpu.VMEM((nf, 3, WIDTH, TILE), BF16),
            pltpu.VMEM((nf, 3, WIDTH, TILE), BF16),
            pltpu.VMEM((width, width), BF16),
            pltpu.VMEM((width, width), BF16),
            pltpu.VMEM((width, width), F32),
            pltpu.VMEM((nf, WIDTH, width), BF16),
            pltpu.VMEM((nf, WIDTH, width), BF16),
            pltpu.VMEM((chips, *piece), BF16),
            pltpu.VMEM((chips, *piece), BF16),
            pltpu.VMEM(piece, BF16),
            pltpu.VMEM((n_dom, *piece), BF16),
            pltpu.SemaphoreType.DMA,
            pltpu.SemaphoreType.DMA((6,)),
            pltpu.SemaphoreType.DMA((16,)),
            pltpu.SemaphoreType.DMA((16,)),
        ],
        compiler_params=pltpu.CompilerParams(
            collective_id=0, has_side_effects=True, vmem_limit_bytes=48 * 2**20
        ),
    )(
        pinned(features),
        pinned(weights),
        pinned(tile_values),
        pinned(tile_blocks.T),
        tile_counts,
        pinned(jnp.swapaxes(replica, 1, 2)),
        pinned(cotangent),
    )


def solution(mesh):
    return jax.shard_map(
        functools.partial(local, mesh.shape["dom"], mesh.shape["feat"]),
        mesh=mesh,
        in_specs=(
            P("feat", "dom"),
            P(),
            P("dom", None, None),
            P("dom", None),
            P("dom"),
            P("dom", None, None),
            P(None, ("dom", "feat")),
        ),
        out_specs=(P(None, ("dom", "feat")), P("feat", "dom"), P(None, "feat", None)),
        check_vma=False,
    )
```

```python
import functools

import jax
import jax.numpy as jnp
from jax import lax
from jax.experimental import pallas as pl
from jax.experimental.pallas import tpu as pltpu
from jax.sharding import PartitionSpec as P

F32 = jnp.float32
BF16 = jnp.bfloat16
TILE = 128
WIDTH = 64
HALF = 8
ROWS = 3 * TILE


def nn(a, b):
    return lax.dot_general(a, b, (((1,), (0,)), ((), ())), preferred_element_type=F32)


def nt(a, b):
    return lax.dot_general(a, b, (((1,), (1,)), ((), ())), preferred_element_type=F32)


def iota(shape, dim):
    return lax.broadcasted_iota(jnp.int32, shape, dim)


def clamp(i, n):
    return jnp.minimum(jnp.maximum(i, 0), n - 1)


def tile_order(seg, src, tiles):
    lane, row = iota((tiles, TILE), 1), iota((tiles, TILE), 0)
    eye = iota((tiles, tiles), 0) == iota((tiles, tiles), 1)
    number = iota((1, tiles), 1)

    def as_col(line):
        return jnp.sum(jnp.where(eye, line, 0), axis=1, keepdims=True)

    key = seg * tiles + number
    seg_col, key_col = as_col(seg), as_col(key)
    rank = jnp.sum(jnp.where(key < key_col, 1, 0), axis=1, keepdims=True)
    begin = jnp.sum(jnp.where(seg < seg_col, 1, 0), axis=1, keepdims=True)
    perm = rank == lane

    def sort(col):
        return jnp.sum(jnp.where(perm, col, 0), axis=0, keepdims=True)

    goes_on = jnp.where(rank == begin, 0, 1)
    last = jnp.sum(jnp.where(seg_col <= lane, 1, 0), axis=0, keepdims=True) - 1
    some = jnp.minimum(jnp.sum(jnp.where(seg_col == lane, 1, 0), axis=0, keepdims=True), 1)
    return [sort(row[:, 0:1]), sort(as_col(src)), sort(goes_on), jnp.maximum(last, 0), some]


def kernel(
    n_dom, nf,
    f_in, w_in, tile_in, tb_in, tc_ref, rep_in, cot_in,
    out_ref, fg_ref, wg_ref,
    f_ref, w_ref, tile_ref, tb_ref, rep_ref, cot_ref,
    loc, loc2, oh, seg, snd, rcv, xbuf, acc, meta_v, meta_s, wt, rows, asend, pre0, pgrad, gsend, ssend, sgr,
    wsend, wpair, wown, wzs, wz, wps, wq, wfin, wall,
    meta_sem, load_sems, ssems, rsems,
):
    me, mf = lax.axis_index("dom"), lax.axis_index("feat")
    ny = n_dom // 8
    chips = n_dom // 2
    my_y, core, chip = me // 8, lax.rem(me, 2), me // 2
    tiles = tile_in.shape[0]
    width = nf * WIDTH
    nmast = 3 * nf
    span = nf * TILE

    loads = [
        pltpu.make_async_copy(src, dst, load_sems.at[i])
        for i, (src, dst) in enumerate(
            (
                (rep_in, rep_ref),
                (f_in, f_ref),
                (tb_in, tb_ref),
                (w_in, w_ref),
                (tile_in, tile_ref),
                (cot_in, cot_ref),
            )
        )
    ]
    for load in loads:
        load.start()

    barrier = pltpu.get_barrier_semaphore()

    def greet_dom(i, _):
        pl.semaphore_signal(barrier, inc=1, device_id={"dom": lax.rem(me + i, n_dom)})
        return 0

    def greet_feat(i, _):
        pl.semaphore_signal(barrier, inc=1, device_id={"feat": lax.rem(mf + i, nf)})
        return 0

    lax.fori_loop(1, n_dom, greet_dom, 0)
    lax.fori_loop(1, nf, greet_feat, 0)

    def dom_copy(src, dst, sem, peer):
        return pltpu.make_async_remote_copy(src, dst, ssems.at[sem], rsems.at[sem], device_id={"dom": peer})

    def feat_copy(src, dst, sem, peer):
        return pltpu.make_async_remote_copy(src, dst, ssems.at[sem], rsems.at[sem], device_id={"feat": peer})

    some_dom, some_feat = lax.rem(me + 1, n_dom), lax.rem(mf + 1, nf)
    my_rows = pl.ds(pl.multiple_of(mf * WIDTH, WIDTH), WIDTH)
    S_F, S_A, S_G, S_S, S_W, S_Z, S_Q, S_L = 4, 5, 8, 11, 12, 13, 14, 15

    def far_first(start, n, step):
        def body(s, _):
            away = n // 2 + ((s + 1) // 2) * (1 - 2 * lax.rem(s, 2))
            step(lax.rem(start + away, n))
            return 0

        lax.fori_loop(0, n, body, 0)

    def rows_of(c):
        return pl.ds(pl.multiple_of(c * TILE, TILE), TILE)

    loads[0].wait()
    loads[1].wait()
    for b in range(nmast):
        loc[b] = f_ref[:, b * TILE : (b + 1) * TILE]

    def build(g, _):
        wide = (8 * HALF, n_dom)
        mine = iota(wide, 1) == g * 8 + (iota(wide, 0) >> 3)
        cols = []
        for h in range(2):
            slots = rep_ref[0, h * HALF : (h + 1) * HALF, :].astype(F32)
            slots = jnp.concatenate([slots] * 8, axis=0)
            cols.append(jnp.sum(jnp.where(mine, slots, 0.0), axis=1, keepdims=True))
        diff = jnp.concatenate(cols, axis=0) - iota((TILE, TILE), 1).astype(F32)
        for r in range(3):
            for f in range(nf):
                at = r * span + f * TILE
                oh[rows_of(g), at : at + TILE] = jnp.where(
                    diff == float((3 * f + r) * TILE), 1.0, 0.0
                ).astype(BF16)
        return 0

    lax.fori_loop(0, ny, build, 0)

    for x in range(4):
        rcv[x, pl.ds(me, 1)] = jnp.zeros((1, HALF, TILE), BF16)

    def chunk(values, r):
        return jnp.concatenate([values[3 * f + r] for f in range(nf)], axis=1)

    def pack(x, g, o):
        side_by_side = jnp.concatenate([o[:64], o[64:]], axis=1)
        snd[x, pl.ds(g * 8, 8)] = side_by_side.reshape(8, HALF, TILE).astype(BF16)

    def send_group(x, g):
        def one(i, _):
            p = g * 8 + i

            @pl.when(p != me)
            def _():
                dom_copy(snd.at[x, p], rcv.at[x, me], x, p).start()

            return 0

        lax.fori_loop(0, 8, one, 0)

    def first_pull(g, _):
        field = jnp.concatenate([chunk(loc, r) for r in range(3)], axis=1)
        pack(0, g, nt(oh[rows_of(g), :], field))
        return 0

    lax.fori_loop(0, ny, first_pull, 0)

    loads[2].wait()
    live = iota((1, tiles), 1) < tc_ref[0]
    source, target = tb_ref[0:1, :], tb_ref[1:2, :]
    table = []
    for to, frm in ((target, source), (source, target)):
        table += tile_order(jnp.where(live, to, nmast + ny), frm, tiles)
    for r, line in enumerate(table):
        meta_v[r : r + 1, :] = line
    meta_copy = pltpu.make_async_copy(meta_v, meta_s, meta_sem)
    meta_copy.start()

    r_i, c_i = iota((TILE, TILE), 0), iota((TILE, TILE), 1)
    place = ((r_i >> 3) & 7) * 16 + (r_i >> 6) * 8 + (r_i & 7)
    perm = jnp.where(place == c_i, 1.0, 0.0).astype(BF16)

    loads[3].wait()
    for k in range(2):
        for a in range(0, width, TILE):
            for b in range(0, width, TILE):
                wt[k, b : b + TILE, a : a + TILE] = jnp.transpose(
                    w_ref[k, a : a + TILE, b : b + TILE].astype(F32)
                ).astype(BF16)
    loads[4].wait()
    loads[5].wait()
    meta_copy.wait()

    pl.semaphore_wait(barrier, n_dom - 1 + nf - 1)

    far_first(my_y, ny, lambda g: send_group(0, g))

    def send_features(j):
        theirs = loc.at[pl.ds(3 * j, 3)]

        @pl.when(j != mf)
        def _():
            feat_copy(theirs, rows.at[0, :, my_rows, :], S_F, j).start()

    far_first(mf, nf, send_features)
    for r in range(3):
        rows[0, r, my_rows, :] = loc[3 * mf + r]

    def await_dom(x):
        dom_copy(snd.at[x, pl.ds(0, n_dom - 1)], rcv.at[x, pl.ds(0, n_dom - 1)], x, some_dom).wait_recv()

    def await_blocks(buf, sem, n):
        feat_copy(buf.at[pl.ds(0, n)], buf.at[pl.ds(0, n)], sem, some_feat).wait_recv()

    def unpacked(x, g):
        t = jnp.transpose(rcv[x, pl.ds(g * 8, 8)].astype(F32).reshape(64, TILE))
        return jnp.concatenate([t[:64], t[64:]], axis=1).astype(BF16)

    def mirrors_in(x, values):
        def body(g, _):
            values[nmast + g] = nn(unpacked(x, g), perm).astype(BF16)
            return 0

        lax.fori_loop(0, ny, body, 0, unroll=True)

    def multiply(values, base, forward, low, high, start):
        def body(j, run):
            lhs = values[clamp(meta_s[base + 1, j], nmast + ny)]
            mat = tile_ref[clamp(meta_s[base, j], tiles)]
            contrib = nn(lhs, mat) if forward else nt(lhs, mat)
            run = run * meta_s[base + 2, j].astype(F32) + contrib
            seg[j] = run
            return run

        return lax.fori_loop(low, high, body, start, unroll=18)

    def partial(base, c):
        return seg[clamp(meta_s[base + 3, c], tiles)] * meta_s[base + 4, c].astype(F32)

    def push(x, base):
        for g in range(ny):
            pack(x, g, nt(perm, partial(base, nmast + g).astype(BF16)))
        far_first(my_y, ny, lambda g: send_group(x, g))

    def mirrors_back(x):
        def body(g, _):
            xbuf[:, rows_of(g)] = unpacked(x, g)
            return 0

        lax.fori_loop(0, ny, body, 0, unroll=True)

    def summed(base, r):
        back = nn(xbuf[...], oh[:, r * span : (r + 1) * span])
        return [partial(base, 3 * f + r) + back[:, f * TILE : (f + 1) * TILE] for f in range(nf)]

    nothing = jnp.zeros((WIDTH, TILE), F32)
    await_dom(0)
    mirrors_in(0, loc)
    multiply(loc, 0, True, 0, tiles, nothing)
    push(1, 0)

    await_blocks(loc, S_F, 3 * (nf - 1))

    def own_half(c, _):
        for r in range(3):
            pre0[r, rows_of(c), :] = nn(wt[0, rows_of(c), :], rows[0, r])
        return 0

    lax.fori_loop(0, width // TILE, own_half, 0)

    await_dom(1)
    mirrors_back(1)

    for r in range(3):

        for f, block in enumerate(summed(0, r)):
            asend[r, f] = block.astype(BF16)

        def send_aggregate(j, r=r):
            @pl.when(j != mf)
            def _():
                feat_copy(asend.at[r, j], rows.at[1, r, my_rows, :], S_A + r, j).start()

        far_first(mf, nf, send_aggregate)
        rows[1, r, my_rows, :] = asend[r, mf]

    for r in range(3):
        await_blocks(asend.at[r], S_A + r, nf - 1)

        cols = slice(r * TILE, (r + 1) * TILE)
        for c in range(width // TILE):
            at = slice(c * TILE, (c + 1) * TILE)
            z = pre0[r, at, :] + nn(wt[1, at, :], rows[1, r])
            s = jax.nn.sigmoid(z)
            out_ref[at, cols] = (z * s).astype(BF16)
            slope = s * (1.0 + z * (1.0 - s))
            pgrad[r, at, :] = (cot_ref[at, cols].astype(F32) * slope).astype(BF16)

        for c in range(width // TILE):
            v = nn(w_ref[1, c * TILE : (c + 1) * TILE, :], pgrad[r]).astype(BF16)
            gsend[r, 2 * c] = v[:WIDTH]
            gsend[r, 2 * c + 1] = v[WIDTH:]

        def send_agg_grad(j, r=r):
            @pl.when(j != mf)
            def _():
                feat_copy(gsend.at[r, j], loc2.at[3 * mf + r], S_G + r, j).start()

            @pl.when(j == mf)
            def _():
                loc2[3 * mf + r] = gsend[r, j]

        far_first(mf, nf, send_agg_grad)

    mate = me + 1 - 2 * core

    def terms(k, c):
        mine = jnp.concatenate([rows[k, r, rows_of(c), :] for r in range(3)], axis=1)
        return nt(mine, jnp.concatenate([pgrad[r] for r in range(3)], axis=1))

    def other_terms(c, _):
        wsend[rows_of(c), :] = terms(1 - core, c).astype(BF16)
        return 0

    lax.fori_loop(0, width // TILE, other_terms, 0, unroll=True)
    dom_copy(wsend, wpair, S_W, mate).start()

    def own_terms(c, _):
        wown[rows_of(c), :] = terms(core, c)
        return 0

    lax.fori_loop(0, width // TILE, own_terms, 0, unroll=True)

    def gathered(g, r):
        return nt(oh[rows_of(g), r * span : (r + 1) * span], chunk(loc2, r))

    def pull_first(g, _):
        acc[g] = gathered(g, 0)
        return 0

    def pull_second(g, _):
        acc[g] = acc[g] + gathered(g, 1)
        return 0

    def pull_last(g):
        pack(2, g, acc[g] + gathered(g, 2))
        send_group(2, g)

    await_blocks(loc2, S_G, nf - 1)
    lax.fori_loop(0, ny, pull_first, 0, unroll=True)

    dom_copy(wsend, wpair, S_W, mate).wait_recv()

    def send_terms(j):
        at = pl.ds(pl.multiple_of(j * WIDTH, WIDTH), WIDTH)
        wzs[j] = (wown[at, :] + wpair[at, :].astype(F32)).astype(BF16)

        @pl.when(j != mf)
        def _():
            feat_copy(wzs.at[j], wz.at[mf], S_Z, j).start()

        @pl.when(j == mf)
        def _():
            wz[mf] = wzs[j]

    far_first(mf, nf, send_terms)

    await_blocks(loc2, S_G + 1, nf - 1)
    lax.fori_loop(0, ny, pull_second, 0, unroll=True)
    await_blocks(loc2, S_G + 2, nf - 1)
    far_first(my_y, ny, pull_last)

    def send_self_grad(j):
        w = w_ref[0, pl.ds(pl.multiple_of(j * WIDTH, WIDTH), WIDTH), :]
        for r in range(3):
            ssend[j, r] = nn(w, pgrad[r]).astype(BF16)

        @pl.when(j != mf)
        def _():
            feat_copy(ssend.at[j], sgr.at[mf], S_S, j).start()

        @pl.when(j == mf)
        def _():
            sgr[mf] = ssend[j]

    far_first(mf, nf, send_self_grad)

    await_dom(2)
    mirrors_in(2, loc2)
    run = multiply(loc2, 5, False, 0, tiles // 2, nothing)

    await_blocks(wz, S_Z, nf - 1)
    pr, pc = WIDTH // ny, width // 4
    total = wz[0].astype(F32)
    for j in range(1, nf):
        total = total + wz[j].astype(F32)
    for y in range(ny):
        for x in range(4):
            wps[4 * y + x] = total[y * pr : (y + 1) * pr, x * pc : (x + 1) * pc].astype(BF16)

    def send_pieces(i, _):
        p = lax.rem(chip + i, chips)
        dom_copy(wps.at[p], wq.at[chip], S_Q, 2 * p + core).start()
        return 0

    lax.fori_loop(1, chips, send_pieces, 0)
    wq[chip] = wps[chip]

    multiply(loc2, 5, False, tiles // 2, tiles, run)
    push(3, 5)

    dom_copy(wq.at[pl.ds(0, chips - 1)], wq.at[pl.ds(0, chips - 1)], S_Q, some_dom).wait_recv()
    whole = wq[0].astype(F32)
    for i in range(1, chips):
        whole = whole + wq[i].astype(F32)
    wfin[...] = whole.astype(BF16)
    wall[me] = whole.astype(BF16)

    def send_final(i, _):
        dom_copy(wfin, wall.at[me], S_L, lax.rem(me + i, n_dom)).start()
        return 0

    lax.fori_loop(1, n_dom, send_final, 0)

    await_blocks(sgr, S_S, nf - 1)
    await_dom(3)
    mirrors_back(3)

    for r in range(3):
        for f, block in enumerate(summed(5, r)):
            at = (3 * f + r) * TILE
            fg_ref[:, at : at + TILE] = (sgr[f, r].astype(F32) + block).astype(BF16)

    dom_copy(wall.at[pl.ds(0, n_dom - 1)], wall.at[pl.ds(0, n_dom - 1)], S_L, some_dom).wait_recv()
    for d in range(n_dom):
        y, x, c = d // 8, (d // 2) % 4, d % 2
        wg_ref[c, y * pr : (y + 1) * pr, x * pc : (x + 1) * pc] = wall[d].astype(F32)

    for x in range(4):
        dom_copy(snd.at[x, pl.ds(0, n_dom - 1)], rcv.at[x, pl.ds(0, n_dom - 1)], x, some_dom).wait_send()

    def drain(buf, sem):
        part = buf.at[pl.ds(0, nf - 1)]
        feat_copy(part, part, sem, some_feat).wait_send()

    for sem, buf in ((S_F, ssend), (S_S, ssend), (S_Z, wzs)):
        drain(buf, sem)
    for r in range(3):
        drain(asend.at[r], S_A + r)
        drain(gsend.at[r], S_G + r)
    dom_copy(wsend, wpair, S_W, mate).wait_send()
    dom_copy(wps.at[pl.ds(0, chips - 1)], wq.at[pl.ds(0, chips - 1)], S_Q, some_dom).wait_send()
    dom_copy(wall.at[pl.ds(0, n_dom - 1)], wall.at[pl.ds(0, n_dom - 1)], S_L, some_dom).wait_send()


def pinned(x):
    return pltpu.with_memory_space_constraint(x, pltpu.HBM)


def local(n_dom, nf, features, weights, tile_values, tile_blocks, tile_counts, replica, cotangent):
    width, tiles = nf * WIDTH, tile_values.shape[0]
    masters = features.shape[1]
    ny, chips = n_dom // 8, n_dom // 2
    nb = 3 * nf + ny
    piece = (WIDTH // ny, width // 4)
    vmem = pl.BlockSpec(memory_space=pltpu.VMEM)
    hbm = pl.BlockSpec(memory_space=pltpu.HBM)
    return pl.pallas_call(
        functools.partial(kernel, n_dom, nf),
        out_shape=(
            jax.ShapeDtypeStruct((width, ROWS), BF16),
            jax.ShapeDtypeStruct((WIDTH, masters), BF16),
            jax.ShapeDtypeStruct((2, WIDTH, width), F32),
        ),
        in_specs=[hbm, hbm, hbm, hbm, pl.BlockSpec(memory_space=pltpu.SMEM), hbm, hbm],
        out_specs=(vmem, vmem, vmem),
        scratch_shapes=[
            pltpu.VMEM((WIDTH, masters), BF16),
            pltpu.VMEM((2, width, width), BF16),
            pltpu.VMEM((tiles, TILE, TILE), BF16),
            pltpu.VMEM((2, tiles), jnp.int32),
            pltpu.VMEM((1, 16, n_dom), jnp.int32),
            pltpu.VMEM((width, ROWS), BF16),
            pltpu.VMEM((nb, WIDTH, TILE), BF16),
            pltpu.VMEM((nb, WIDTH, TILE), BF16),
            pltpu.VMEM((n_dom * 16, masters), BF16),
            pltpu.VMEM((tiles, WIDTH, TILE), F32),
            pltpu.VMEM((4, n_dom, HALF, TILE), BF16),
            pltpu.VMEM((4, n_dom, HALF, TILE), BF16),
            pltpu.VMEM((WIDTH, n_dom * 16), BF16),
            pltpu.VMEM((ny, TILE, WIDTH), F32),
            pltpu.VMEM((16, TILE), jnp.int32),
            pltpu.SMEM((16, TILE), jnp.int32),
            pltpu.VMEM((2, width, width), BF16),
            pltpu.VMEM((2, 3, width, TILE), BF16),
            pltpu.VMEM((3, nf, WIDTH, TILE), BF16),
            pltpu.VMEM((3, width, TILE), F32),
            pltpu.VMEM((3, width, TILE), BF16),
            pltpu.VMEM((3, nf, WIDTH, TILE), BF16),
            pltpu.VMEM((nf, 3, WIDTH, TILE), BF16),
            pltpu.VMEM((nf, 3, WIDTH, TILE), BF16),
            pltpu.VMEM((width, width), BF16),
            pltpu.VMEM((width, width), BF16),
            pltpu.VMEM((width, width), F32),
            pltpu.VMEM((nf, WIDTH, width), BF16),
            pltpu.VMEM((nf, WIDTH, width), BF16),
            pltpu.VMEM((chips, *piece), BF16),
            pltpu.VMEM((chips, *piece), BF16),
            pltpu.VMEM(piece, BF16),
            pltpu.VMEM((n_dom, *piece), BF16),
            pltpu.SemaphoreType.DMA,
            pltpu.SemaphoreType.DMA((6,)),
            pltpu.SemaphoreType.DMA((16,)),
            pltpu.SemaphoreType.DMA((16,)),
        ],
        compiler_params=pltpu.CompilerParams(
            collective_id=0, has_side_effects=True, vmem_limit_bytes=48 * 2**20
        ),
    )(
        pinned(features),
        pinned(weights),
        pinned(tile_values),
        pinned(tile_blocks.T),
        tile_counts,
        pinned(jnp.swapaxes(replica, 1, 2)),
        pinned(cotangent),
    )


def solution(mesh):
    return jax.shard_map(
        functools.partial(local, mesh.shape["dom"], mesh.shape["feat"]),
        mesh=mesh,
        in_specs=(
            P("feat", "dom"),
            P(),
            P("dom", None, None),
            P("dom", None),
            P("dom"),
            P("dom", None, None),
            P(None, ("dom", "feat")),
        ),
        out_specs=(P(None, ("dom", "feat")), P("feat", "dom"), P(None, "feat", None)),
        check_vma=False,
    )
```

```python
import functools

import jax
import jax.numpy as jnp
from jax import lax
from jax.experimental import pallas as pl
from jax.experimental.pallas import tpu as pltpu
from jax.sharding import PartitionSpec as P

F32 = jnp.float32
BF16 = jnp.bfloat16
TILE = 128
WIDTH = 64
HALF = 8
ROWS = 3 * TILE


def nn(a, b):
    return lax.dot_general(a, b, (((1,), (0,)), ((), ())), preferred_element_type=F32)


def nt(a, b):
    return lax.dot_general(a, b, (((1,), (1,)), ((), ())), preferred_element_type=F32)


def iota(shape, dim):
    return lax.broadcasted_iota(jnp.int32, shape, dim)


def clamp(i, n):
    return jnp.minimum(jnp.maximum(i, 0), n - 1)


def tile_order(seg, src, tiles):
    lane, row = iota((tiles, TILE), 1), iota((tiles, TILE), 0)
    eye = iota((tiles, tiles), 0) == iota((tiles, tiles), 1)
    number = iota((1, tiles), 1)

    def as_col(line):
        return jnp.sum(jnp.where(eye, line, 0), axis=1, keepdims=True)

    key = seg * tiles + number
    seg_col, key_col = as_col(seg), as_col(key)
    rank = jnp.sum(jnp.where(key < key_col, 1, 0), axis=1, keepdims=True)
    begin = jnp.sum(jnp.where(seg < seg_col, 1, 0), axis=1, keepdims=True)
    perm = rank == lane

    def sort(col):
        return jnp.sum(jnp.where(perm, col, 0), axis=0, keepdims=True)

    goes_on = jnp.where(rank == begin, 0, 1)
    last = jnp.sum(jnp.where(seg_col <= lane, 1, 0), axis=0, keepdims=True) - 1
    some = jnp.minimum(jnp.sum(jnp.where(seg_col == lane, 1, 0), axis=0, keepdims=True), 1)
    return [sort(row[:, 0:1]), sort(as_col(src)), sort(goes_on), jnp.maximum(last, 0), some]


def kernel(
    n_dom, nf,
    f_in, w_in, tile_in, tb_in, tc_ref, rep_in, cot_in,
    out_ref, fg_ref, wg_ref,
    f_ref, w_ref, tile_ref, tb_ref, rep_ref, cot_ref,
    loc, loc2, oh, seg, snd, rcv, xbuf, acc, meta_v, meta_s, wt, rows, asend, pre0, pgrad, gsend, ssend, sgr,
    wsend, wpair, wown, wzs, wz, wps, wq, wfin, wall,
    meta_sem, load_sems, ssems, rsems,
):
    me, mf = lax.axis_index("dom"), lax.axis_index("feat")
    ny = n_dom // 8
    chips = n_dom // 2
    my_y, core, chip = me // 8, lax.rem(me, 2), me // 2
    tiles = tile_in.shape[0]
    width = nf * WIDTH
    nmast = 3 * nf
    span = nf * TILE

    loads = [
        pltpu.make_async_copy(src, dst, load_sems.at[i])
        for i, (src, dst) in enumerate(
            (
                (rep_in, rep_ref),
                (f_in, f_ref),
                (tb_in, tb_ref),
                (w_in, w_ref),
                (tile_in, tile_ref),
                (cot_in, cot_ref),
            )
        )
    ]
    for load in loads:
        load.start()

    barrier = pltpu.get_barrier_semaphore()

    def greet_dom(i, _):
        pl.semaphore_signal(barrier, inc=1, device_id={"dom": lax.rem(me + i, n_dom)})
        return 0

    def greet_feat(i, _):
        pl.semaphore_signal(barrier, inc=1, device_id={"feat": lax.rem(mf + i, nf)})
        return 0

    lax.fori_loop(1, n_dom, greet_dom, 0)
    lax.fori_loop(1, nf, greet_feat, 0)

    def dom_copy(src, dst, sem, peer):
        return pltpu.make_async_remote_copy(src, dst, ssems.at[sem], rsems.at[sem], device_id={"dom": peer})

    def feat_copy(src, dst, sem, peer):
        return pltpu.make_async_remote_copy(src, dst, ssems.at[sem], rsems.at[sem], device_id={"feat": peer})

    some_dom, some_feat = lax.rem(me + 1, n_dom), lax.rem(mf + 1, nf)
    my_rows = pl.ds(pl.multiple_of(mf * WIDTH, WIDTH), WIDTH)
    S_F, S_A, S_G, S_S, S_W, S_Z, S_Q, S_L = 4, 5, 8, 11, 12, 13, 14, 15

    def far_first(start, n, step):
        def body(s, _):
            away = n // 2 + ((s + 1) // 2) * (1 - 2 * lax.rem(s, 2))
            step(lax.rem(start + away, n))
            return 0

        lax.fori_loop(0, n, body, 0)

    def rows_of(c):
        return pl.ds(pl.multiple_of(c * TILE, TILE), TILE)

    loads[0].wait()
    loads[1].wait()
    for b in range(nmast):
        loc[b] = f_ref[:, b * TILE : (b + 1) * TILE]

    def build(g, _):
        wide = (8 * HALF, n_dom)
        mine = iota(wide, 1) == g * 8 + (iota(wide, 0) >> 3)
        cols = []
        for h in range(2):
            slots = rep_ref[0, h * HALF : (h + 1) * HALF, :].astype(F32)
            slots = jnp.concatenate([slots] * 8, axis=0)
            cols.append(jnp.sum(jnp.where(mine, slots, 0.0), axis=1, keepdims=True))
        diff = jnp.concatenate(cols, axis=0) - iota((TILE, TILE), 1).astype(F32)
        for r in range(3):
            for f in range(nf):
                at = r * span + f * TILE
                oh[rows_of(g), at : at + TILE] = jnp.where(
                    diff == float((3 * f + r) * TILE), 1.0, 0.0
                ).astype(BF16)
        return 0

    lax.fori_loop(0, ny, build, 0)

    for x in range(4):
        rcv[x, pl.ds(me, 1)] = jnp.zeros((1, HALF, TILE), BF16)

    def chunk(values, r):
        return jnp.concatenate([values[3 * f + r] for f in range(nf)], axis=1)

    def pack(x, g, o):
        side_by_side = jnp.concatenate([o[:64], o[64:]], axis=1)
        snd[x, pl.ds(g * 8, 8)] = side_by_side.reshape(8, HALF, TILE).astype(BF16)

    def send_group(x, g):
        def one(i, _):
            p = g * 8 + i

            @pl.when(p != me)
            def _():
                dom_copy(snd.at[x, p], rcv.at[x, me], x, p).start()

            return 0

        lax.fori_loop(0, 8, one, 0)

    def first_pull(g, _):
        field = jnp.concatenate([chunk(loc, r) for r in range(3)], axis=1)
        pack(0, g, nt(oh[rows_of(g), :], field))
        return 0

    lax.fori_loop(0, ny, first_pull, 0)

    loads[2].wait()
    live = iota((1, tiles), 1) < tc_ref[0]
    source, target = tb_ref[0:1, :], tb_ref[1:2, :]
    table = []
    for to, frm in ((target, source), (source, target)):
        table += tile_order(jnp.where(live, to, nmast + ny), frm, tiles)
    for r, line in enumerate(table):
        meta_v[r : r + 1, :] = line
    meta_copy = pltpu.make_async_copy(meta_v, meta_s, meta_sem)
    meta_copy.start()

    r_i, c_i = iota((TILE, TILE), 0), iota((TILE, TILE), 1)
    place = ((r_i >> 3) & 7) * 16 + (r_i >> 6) * 8 + (r_i & 7)
    perm = jnp.where(place == c_i, 1.0, 0.0).astype(BF16)

    loads[3].wait()
    for k in range(2):
        for a in range(0, width, TILE):
            for b in range(0, width, TILE):
                wt[k, b : b + TILE, a : a + TILE] = jnp.transpose(
                    w_ref[k, a : a + TILE, b : b + TILE].astype(F32)
                ).astype(BF16)
    loads[4].wait()
    loads[5].wait()
    meta_copy.wait()

    pl.semaphore_wait(barrier, n_dom - 1 + nf - 1)

    far_first(my_y, ny, lambda g: send_group(0, g))

    def send_features(j):
        theirs = loc.at[pl.ds(3 * j, 3)]

        @pl.when(j != mf)
        def _():
            feat_copy(theirs, rows.at[0, :, my_rows, :], S_F, j).start()

    far_first(mf, nf, send_features)
    for r in range(3):
        rows[0, r, my_rows, :] = loc[3 * mf + r]

    def await_dom(x):
        dom_copy(snd.at[x, pl.ds(0, n_dom - 1)], rcv.at[x, pl.ds(0, n_dom - 1)], x, some_dom).wait_recv()

    def await_blocks(buf, sem, n):
        feat_copy(buf.at[pl.ds(0, n)], buf.at[pl.ds(0, n)], sem, some_feat).wait_recv()

    def unpacked(x, g):
        t = jnp.transpose(rcv[x, pl.ds(g * 8, 8)].astype(F32).reshape(64, TILE))
        return jnp.concatenate([t[:64], t[64:]], axis=1).astype(BF16)

    def mirrors_in(x, values):
        def body(g, _):
            values[nmast + g] = nn(unpacked(x, g), perm).astype(BF16)
            return 0

        lax.fori_loop(0, ny, body, 0, unroll=True)

    def multiply(values, base, forward, low, high, start):
        def body(j, run):
            lhs = values[clamp(meta_s[base + 1, j], nmast + ny)]
            mat = tile_ref[clamp(meta_s[base, j], tiles)]
            contrib = nn(lhs, mat) if forward else nt(lhs, mat)
            run = run * meta_s[base + 2, j].astype(F32) + contrib
            seg[j] = run
            return run

        return lax.fori_loop(low, high, body, start, unroll=18)

    def partial(base, c):
        return seg[clamp(meta_s[base + 3, c], tiles)] * meta_s[base + 4, c].astype(F32)

    def push(x, base):
        for g in range(ny):
            pack(x, g, nt(perm, partial(base, nmast + g).astype(BF16)))
        far_first(my_y, ny, lambda g: send_group(x, g))

    def mirrors_back(x):
        def body(g, _):
            xbuf[:, rows_of(g)] = unpacked(x, g)
            return 0

        lax.fori_loop(0, ny, body, 0, unroll=True)

    def summed(base, r):
        back = nn(xbuf[...], oh[:, r * span : (r + 1) * span])
        return [partial(base, 3 * f + r) + back[:, f * TILE : (f + 1) * TILE] for f in range(nf)]

    nothing = jnp.zeros((WIDTH, TILE), F32)
    await_dom(0)
    mirrors_in(0, loc)
    multiply(loc, 0, True, 0, tiles, nothing)
    push(1, 0)

    await_blocks(loc, S_F, 3 * (nf - 1))

    def own_half(c, _):
        for r in range(3):
            pre0[r, rows_of(c), :] = nn(wt[0, rows_of(c), :], rows[0, r])
        return 0

    lax.fori_loop(0, width // TILE, own_half, 0)

    await_dom(1)
    mirrors_back(1)

    for r in range(3):

        for f, block in enumerate(summed(0, r)):
            asend[r, f] = block.astype(BF16)

        def send_aggregate(j, r=r):
            @pl.when(j != mf)
            def _():
                feat_copy(asend.at[r, j], rows.at[1, r, my_rows, :], S_A + r, j).start()

        far_first(mf, nf, send_aggregate)
        rows[1, r, my_rows, :] = asend[r, mf]

    for r in range(3):
        await_blocks(asend.at[r], S_A + r, nf - 1)

        cols = slice(r * TILE, (r + 1) * TILE)
        for c in range(width // TILE):
            at = slice(c * TILE, (c + 1) * TILE)
            z = pre0[r, at, :] + nn(wt[1, at, :], rows[1, r])
            s = jax.nn.sigmoid(z)
            out_ref[at, cols] = (z * s).astype(BF16)
            slope = s * (1.0 + z * (1.0 - s))
            pgrad[r, at, :] = (cot_ref[at, cols].astype(F32) * slope).astype(BF16)

        for c in range(width // TILE):
            v = nn(w_ref[1, c * TILE : (c + 1) * TILE, :], pgrad[r]).astype(BF16)
            gsend[r, 2 * c] = v[:WIDTH]
            gsend[r, 2 * c + 1] = v[WIDTH:]

        def send_agg_grad(j, r=r):
            @pl.when(j != mf)
            def _():
                feat_copy(gsend.at[r, j], loc2.at[3 * mf + r], S_G + r, j).start()

            @pl.when(j == mf)
            def _():
                loc2[3 * mf + r] = gsend[r, j]

        far_first(mf, nf, send_agg_grad)

    mate = me + 1 - 2 * core

    def terms(k, c):
        mine = jnp.concatenate([rows[k, r, rows_of(c), :] for r in range(3)], axis=1)
        return nt(mine, jnp.concatenate([pgrad[r] for r in range(3)], axis=1))

    def other_terms(c, _):
        wsend[rows_of(c), :] = terms(1 - core, c).astype(BF16)
        return 0

    lax.fori_loop(0, width // TILE, other_terms, 0, unroll=True)
    dom_copy(wsend, wpair, S_W, mate).start()

    def own_terms(c, _):
        wown[rows_of(c), :] = terms(core, c)
        return 0

    lax.fori_loop(0, width // TILE, own_terms, 0, unroll=True)

    dom_copy(wsend, wpair, S_W, mate).wait_recv()

    def send_terms(j):
        at = pl.ds(pl.multiple_of(j * WIDTH, WIDTH), WIDTH)
        wzs[j] = (wown[at, :] + wpair[at, :].astype(F32)).astype(BF16)

        @pl.when(j != mf)
        def _():
            feat_copy(wzs.at[j], wz.at[mf], S_Z, j).start()

        @pl.when(j == mf)
        def _():
            wz[mf] = wzs[j]

    far_first(mf, nf, send_terms)

    def gathered(g, r):
        return nt(oh[rows_of(g), r * span : (r + 1) * span], chunk(loc2, r))

    def pull_first(g, _):
        acc[g] = gathered(g, 0)
        return 0

    def pull_second(g, _):
        acc[g] = acc[g] + gathered(g, 1)
        return 0

    def pull_last(g):
        pack(2, g, acc[g] + gathered(g, 2))
        send_group(2, g)

    await_blocks(loc2, S_G, nf - 1)
    lax.fori_loop(0, ny, pull_first, 0, unroll=True)

    await_blocks(loc2, S_G + 1, nf - 1)
    lax.fori_loop(0, ny, pull_second, 0, unroll=True)
    await_blocks(loc2, S_G + 2, nf - 1)
    far_first(my_y, ny, pull_last)

    for c in range(width // TILE):
        for r in range(3):
            v = nn(w_ref[0, c * TILE : (c + 1) * TILE, :], pgrad[r]).astype(BF16)
            ssend[2 * c, r] = v[:WIDTH]
            ssend[2 * c + 1, r] = v[WIDTH:]
    sgr[mf] = ssend[mf]

    def send_self_grad(j):
        @pl.when(j != mf)
        def _():
            feat_copy(ssend.at[j], sgr.at[mf], S_S, j).start()

    await_dom(2)
    mirrors_in(2, loc2)
    run = multiply(loc2, 5, False, 0, tiles // 2, nothing)

    await_blocks(wz, S_Z, nf - 1)
    pr, pc = WIDTH // ny, width // 4
    total = wz[0].astype(F32)
    for j in range(1, nf):
        total = total + wz[j].astype(F32)
    for y in range(ny):
        for x in range(4):
            wps[4 * y + x] = total[y * pr : (y + 1) * pr, x * pc : (x + 1) * pc].astype(BF16)

    def send_pieces(i, _):
        p = lax.rem(chip + i, chips)
        dom_copy(wps.at[p], wq.at[chip], S_Q, 2 * p + core).start()
        return 0

    lax.fori_loop(1, chips, send_pieces, 0)
    wq[chip] = wps[chip]

    far_first(mf, nf, send_self_grad)
    multiply(loc2, 5, False, tiles // 2, tiles, run)
    push(3, 5)

    dom_copy(wq.at[pl.ds(0, chips - 1)], wq.at[pl.ds(0, chips - 1)], S_Q, some_dom).wait_recv()
    whole = wq[0].astype(F32)
    for i in range(1, chips):
        whole = whole + wq[i].astype(F32)
    wfin[...] = whole.astype(BF16)
    wall[me] = whole.astype(BF16)

    def send_final(i, _):
        dom_copy(wfin, wall.at[me], S_L, lax.rem(me + i, n_dom)).start()
        return 0

    lax.fori_loop(1, n_dom, send_final, 0)

    await_blocks(sgr, S_S, nf - 1)
    await_dom(3)
    mirrors_back(3)

    for r in range(3):
        for f, block in enumerate(summed(5, r)):
            at = (3 * f + r) * TILE
            fg_ref[:, at : at + TILE] = (sgr[f, r].astype(F32) + block).astype(BF16)

    dom_copy(wall.at[pl.ds(0, n_dom - 1)], wall.at[pl.ds(0, n_dom - 1)], S_L, some_dom).wait_recv()
    for d in range(n_dom):
        y, x, c = d // 8, (d // 2) % 4, d % 2
        wg_ref[c, y * pr : (y + 1) * pr, x * pc : (x + 1) * pc] = wall[d].astype(F32)

    for x in range(4):
        dom_copy(snd.at[x, pl.ds(0, n_dom - 1)], rcv.at[x, pl.ds(0, n_dom - 1)], x, some_dom).wait_send()

    def drain(buf, sem):
        part = buf.at[pl.ds(0, nf - 1)]
        feat_copy(part, part, sem, some_feat).wait_send()

    for sem, buf in ((S_F, ssend), (S_S, ssend), (S_Z, wzs)):
        drain(buf, sem)
    for r in range(3):
        drain(asend.at[r], S_A + r)
        drain(gsend.at[r], S_G + r)
    dom_copy(wsend, wpair, S_W, mate).wait_send()
    dom_copy(wps.at[pl.ds(0, chips - 1)], wq.at[pl.ds(0, chips - 1)], S_Q, some_dom).wait_send()
    dom_copy(wall.at[pl.ds(0, n_dom - 1)], wall.at[pl.ds(0, n_dom - 1)], S_L, some_dom).wait_send()


def pinned(x):
    return pltpu.with_memory_space_constraint(x, pltpu.HBM)


def local(n_dom, nf, features, weights, tile_values, tile_blocks, tile_counts, replica, cotangent):
    width, tiles = nf * WIDTH, tile_values.shape[0]
    masters = features.shape[1]
    ny, chips = n_dom // 8, n_dom // 2
    nb = 3 * nf + ny
    piece = (WIDTH // ny, width // 4)
    vmem = pl.BlockSpec(memory_space=pltpu.VMEM)
    hbm = pl.BlockSpec(memory_space=pltpu.HBM)
    return pl.pallas_call(
        functools.partial(kernel, n_dom, nf),
        out_shape=(
            jax.ShapeDtypeStruct((width, ROWS), BF16),
            jax.ShapeDtypeStruct((WIDTH, masters), BF16),
            jax.ShapeDtypeStruct((2, WIDTH, width), F32),
        ),
        in_specs=[hbm, hbm, hbm, hbm, pl.BlockSpec(memory_space=pltpu.SMEM), hbm, hbm],
        out_specs=(vmem, vmem, vmem),
        scratch_shapes=[
            pltpu.VMEM((WIDTH, masters), BF16),
            pltpu.VMEM((2, width, width), BF16),
            pltpu.VMEM((tiles, TILE, TILE), BF16),
            pltpu.VMEM((2, tiles), jnp.int32),
            pltpu.VMEM((1, 16, n_dom), jnp.int32),
            pltpu.VMEM((width, ROWS), BF16),
            pltpu.VMEM((nb, WIDTH, TILE), BF16),
            pltpu.VMEM((nb, WIDTH, TILE), BF16),
            pltpu.VMEM((n_dom * 16, masters), BF16),
            pltpu.VMEM((tiles, WIDTH, TILE), F32),
            pltpu.VMEM((4, n_dom, HALF, TILE), BF16),
            pltpu.VMEM((4, n_dom, HALF, TILE), BF16),
            pltpu.VMEM((WIDTH, n_dom * 16), BF16),
            pltpu.VMEM((ny, TILE, WIDTH), F32),
            pltpu.VMEM((16, TILE), jnp.int32),
            pltpu.SMEM((16, TILE), jnp.int32),
            pltpu.VMEM((2, width, width), BF16),
            pltpu.VMEM((2, 3, width, TILE), BF16),
            pltpu.VMEM((3, nf, WIDTH, TILE), BF16),
            pltpu.VMEM((3, width, TILE), F32),
            pltpu.VMEM((3, width, TILE), BF16),
            pltpu.VMEM((3, nf, WIDTH, TILE), BF16),
            pltpu.VMEM((nf, 3, WIDTH, TILE), BF16),
            pltpu.VMEM((nf, 3, WIDTH, TILE), BF16),
            pltpu.VMEM((width, width), BF16),
            pltpu.VMEM((width, width), BF16),
            pltpu.VMEM((width, width), F32),
            pltpu.VMEM((nf, WIDTH, width), BF16),
            pltpu.VMEM((nf, WIDTH, width), BF16),
            pltpu.VMEM((chips, *piece), BF16),
            pltpu.VMEM((chips, *piece), BF16),
            pltpu.VMEM(piece, BF16),
            pltpu.VMEM((n_dom, *piece), BF16),
            pltpu.SemaphoreType.DMA,
            pltpu.SemaphoreType.DMA((6,)),
            pltpu.SemaphoreType.DMA((16,)),
            pltpu.SemaphoreType.DMA((16,)),
        ],
        compiler_params=pltpu.CompilerParams(
            collective_id=0, has_side_effects=True, vmem_limit_bytes=48 * 2**20
        ),
    )(
        pinned(features),
        pinned(weights),
        pinned(tile_values),
        pinned(tile_blocks.T),
        tile_counts,
        pinned(jnp.swapaxes(replica, 1, 2)),
        pinned(cotangent),
    )


def solution(mesh):
    return jax.shard_map(
        functools.partial(local, mesh.shape["dom"], mesh.shape["feat"]),
        mesh=mesh,
        in_specs=(
            P("feat", "dom"),
            P(),
            P("dom", None, None),
            P("dom", None),
            P("dom"),
            P("dom", None, None),
            P(None, ("dom", "feat")),
        ),
        out_specs=(P(None, ("dom", "feat")), P("feat", "dom"), P(None, "feat", None)),
        check_vma=False,
    )
```
